32 devices in a mesh: groups: 2 (over y), vocab: 4 (over z), rows: 4 (over x, core).
Axes of the slice: x: 2, y: 2, z: 4, core: 2. Of those that a mesh axis runs over, the one named last changes fastest.
Arguments:
- llama_logits: bfloat16 [1024, 8192], P(('groups', 'rows'), 'vocab'), parts along dimension 0, may hold values from -64 to 620
- qwen_logits: bfloat16 [1024, 9728], P(('groups', 'rows'), 'vocab'), parts along dimension 0, may hold values from -64 to 620
- gemma_logits: bfloat16 [1024, 16384], P(('groups', 'rows'), 'vocab'), parts along dimension 0, may hold values from -64 to 620
- student_logits: bfloat16 [1024, 8192], P(('groups', 'rows'), 'vocab'), parts along dimension 0, may hold values from -64 to 620
- align_llama: int32 [128, 3], P('vocab'), may hold values from 0 to 63, as said below
- align_qwen: int32 [152, 3], P('vocab'), may hold values from 0 to 75, as said below
- align_gemma: int32 [256, 3], P('vocab'), may hold values from 0 to 127, as said below
- tiles: bfloat16 [16, 128, 128], replicated, as said below
- student_order: int32 [64], replicated, may hold values from 0 to 63, as said below
Outputs:
- row_loss: float32 [1024], P(('groups', 'rows')), parts along dimension 0
- grad: bfloat16 [1024, 8192], P(('groups', 'rows'), 'vocab'), parts along dimension 0
The draws below stay inside these ranges and needn't reach their ends.
There are 2 independent parts, one for each index of `groups`. The reference program is written for one: setup_inputs(seed, part) draws one part's arguments, and reference() takes and returns one part's arrays. A program takes and returns all parts, laid end to end along the dimension named above; an argument that names none is the same for every part. Nothing has to cross between parts.
Inputs may be any that keep to these rules, and one draw needn't show every extreme that they name: `align_llama`: row e of block i of 32 rows names teacher block i * 16 + e // 2; column 1 is a student vocabulary block, column 2 a tile. Over the three lists, the rows of one block i name at most 4 different student blocks whose column block lies in any one range j * 16 to (j + 1) * 16 - 1 of position; for one range j this many from every block i. `align_qwen`: row e of block i of 38 rows names teacher block i * 19 + e // 2; columns as in align_llama, under the same bound. `align_gemma`: row e of block i of 64 rows names teacher block i * 32 + e // 2; columns as in align_llama, under the same bound. `student_order`: a permutation. `tiles`: nonnegative.
All inputs are finite; a program needn't handle non-finite values.
Results may differ from the reference program's by a relative error of at most 0.0041.
Values may be sent and summed in bfloat16 or wider, within the bound.
A program may use at most 128 MiB of HBM per device.

```python
import jax
import jax.numpy as jnp
from jax import lax

ROW_DEV = 128
ROWS = 512
BLK = 128
LLAMA_BLK = 16
QWEN_BLK = 19
GEMMA_BLK = 32
STUDENT_BLK = 16
LLAMA_V = 8192
QWEN_V = 9728
GEMMA_V = 16384
STUDENT_V = 8192
STUDENT_BLOCKS = 64
EPB = 2
CAP = 4
NTILE = 16
N_VOCAB = 4
N_ROWS = 4


def shared_tables(key):
    order = jax.random.permutation(jax.random.fold_in(key, 101), STUDENT_BLOCKS).astype(jnp.int32)
    turns = jax.random.randint(jax.random.fold_in(key, 102), (N_VOCAB, N_VOCAB), 0, STUDENT_BLK)
    hot_owner = jax.random.randint(jax.random.fold_in(key, 103), (), 0, N_VOCAB)
    return (order, turns, hot_owner)


def alignment_rows(base_key, own_key, blocks, forced):
    order, turns, hot_owner = shared_tables(base_key)
    count = EPB * blocks
    index = jnp.arange(N_VOCAB * count, dtype=jnp.int32)
    source = index // count
    local = index % count
    owner = jax.random.randint(jax.random.fold_in(own_key, 1), index.shape, 0, N_VOCAB)
    offset = jax.random.randint(jax.random.fold_in(own_key, 2), index.shape, 0, CAP)
    if forced:
        owner = jnp.where(local < CAP, hot_owner, owner)
        offset = jnp.where(local < CAP, local, offset)
    column_block = owner * STUDENT_BLK + (offset + turns[source, owner]) % STUDENT_BLK
    tile_index = jax.random.randint(jax.random.fold_in(own_key, 3), index.shape, 0, NTILE)
    teacher_block = source * blocks + local // EPB
    return jnp.stack([teacher_block, order[column_block], tile_index], axis=1).astype(jnp.int32)


def draw_align_llama(key, part):
    own_key = jax.random.fold_in(key, 11)
    return alignment_rows(key, own_key, LLAMA_BLK, True)


def draw_align_qwen(key, part):
    own_key = jax.random.fold_in(key, 12)
    return alignment_rows(key, own_key, QWEN_BLK, False)


def draw_align_gemma(key, part):
    own_key = jax.random.fold_in(key, 13)
    return alignment_rows(key, own_key, GEMMA_BLK, False)


def draw_student_order(key, part):
    order, turns, hot_owner = shared_tables(key)
    return order


def draw_tiles(key, part):
    key = jax.random.fold_in(key, 21)
    identity = jnp.eye(BLK, dtype=jnp.float32)
    spread = jax.random.uniform(key, (NTILE, BLK, BLK), minval=0.0, maxval=2.0)
    values = identity + spread / BLK
    return (values * (1.0 / (2.0 * EPB))).astype(jnp.bfloat16)


def spread_field(key, height, width, scale):
    return jnp.clip(scale * jax.random.normal(key, (height, width), jnp.float32), -8.0 * scale, 8.0 * scale)


def draw_llama_logits(key, part):
    key = jax.random.fold_in(key, 31)
    values = spread_field(key, ROWS, LLAMA_V, 3.0)
    return values.astype(jnp.bfloat16)


def draw_qwen_logits(key, part):
    key = jax.random.fold_in(key, 32)
    values = spread_field(key, ROWS, QWEN_V, 3.0)
    return values.astype(jnp.bfloat16)


def draw_gemma_logits(key, part):
    key = jax.random.fold_in(key, 33)
    values = spread_field(key, ROWS, GEMMA_V, 3.0)
    return values.astype(jnp.bfloat16)


def draw_student_logits(key, part):
    key = jax.random.fold_in(key, 34)
    row_shift = jax.random.uniform(jax.random.fold_in(key, 9), (ROWS, 1), minval=0.0, maxval=40.0)
    values = spread_field(key, ROWS, STUDENT_V, 2.0) + row_shift
    return values.astype(jnp.bfloat16)


def setup_inputs(seed: int = 0, part: int = 0) -> dict:
    seeds = jax.random.split(jax.random.key(seed), 10)
    part_keys = jax.random.split(jax.random.fold_in(seeds[9], part), 10)
    return {
        "llama_logits": draw_llama_logits(jax.random.fold_in(jax.random.fold_in(seeds[9], part), 71), part),
        "qwen_logits": draw_qwen_logits(jax.random.fold_in(jax.random.fold_in(seeds[9], part), 71), part),
        "gemma_logits": draw_gemma_logits(jax.random.fold_in(jax.random.fold_in(seeds[9], part), 71), part),
        "student_logits": draw_student_logits(jax.random.fold_in(jax.random.fold_in(seeds[9], part), 71), part),
        "align_llama": draw_align_llama(jax.random.fold_in(seeds[9], 71), part),
        "align_qwen": draw_align_qwen(jax.random.fold_in(seeds[9], 71), part),
        "align_gemma": draw_align_gemma(jax.random.fold_in(seeds[9], 71), part),
        "tiles": draw_tiles(jax.random.fold_in(seeds[9], 71), part),
        "student_order": draw_student_order(jax.random.fold_in(seeds[9], 71), part),
    }


TEMP = 2.0
SHARE = 1.0 / 3.0


def probabilities(logits):
    scaled = logits.astype(jnp.float32) / TEMP
    highest = jnp.max(scaled, axis=1, keepdims=True)
    weights = jnp.exp(scaled - highest)
    return (weights / jnp.sum(weights, axis=1, keepdims=True)).astype(jnp.bfloat16)


def group_partial(probs_list, lists, counts, tiles, position, group):
    width = probs_list[0].shape[0]
    partial_sum = jnp.zeros((STUDENT_BLOCKS, width, BLK), jnp.float32)
    for probs, align, count in zip(probs_list, lists, counts):
        entry_rows = lax.dynamic_slice_in_dim(align, (group * count).astype(jnp.int32), count, 0)
        grid = probs.reshape(width, probs.shape[1] // BLK, BLK)
        picked = jnp.take(grid, entry_rows[:, 0], axis=1).astype(jnp.float32)
        tile_rows = jnp.take(tiles, entry_rows[:, 2], axis=0).astype(jnp.float32)
        mapped_part = jnp.einsum("reb,ebc->erc", picked, tile_rows) * SHARE
        partial_sum = partial_sum + jax.ops.segment_sum(mapped_part, position[entry_rows[:, 1]], num_segments=STUDENT_BLOCKS)
    return partial_sum


def reference(llama_logits, qwen_logits, gemma_logits, student_logits, align_llama, align_qwen, align_gemma, tiles, student_order):
    position = jnp.zeros((STUDENT_BLOCKS,), jnp.int32).at[student_order].set(jnp.arange(STUDENT_BLOCKS, dtype=jnp.int32))
    lists = (align_llama, align_qwen, align_gemma)
    counts = (EPB * LLAMA_BLK, EPB * QWEN_BLK, EPB * GEMMA_BLK)

    def one_block(start):
        def rows_of(values):
            return lax.dynamic_slice_in_dim(values, start, ROW_DEV, 0)

        probs_list = [probabilities(rows_of(values)) for values in (llama_logits, qwen_logits, gemma_logits)]

        def add_group(group, target):
            partial_sum = group_partial(probs_list, lists, counts, tiles, position, group)
            rounded = lax.optimization_barrier(partial_sum.astype(jnp.bfloat16))
            return target + rounded.astype(jnp.float32)

        target = lax.fori_loop(0, N_VOCAB, add_group, jnp.zeros((STUDENT_BLOCKS, ROW_DEV, BLK), jnp.float32))
        target = jnp.transpose(target, (1, 0, 2)).reshape(ROW_DEV, STUDENT_BLOCKS * BLK)
        scaled = rows_of(student_logits).astype(jnp.float32) / TEMP
        highest = jnp.max(scaled, axis=1, keepdims=True)
        lse = highest + jnp.log(jnp.sum(jnp.exp(scaled - highest), axis=1, keepdims=True))
        total = jnp.sum(target, axis=1, keepdims=True)
        row_loss = total[:, 0] * lse[:, 0] - jnp.sum(target * scaled, axis=1)
        factor = STUDENT_BLOCKS * BLK / TEMP
        grad = (factor * (total * jnp.exp(scaled - lse) - target)).astype(jnp.bfloat16)
        return row_loss, grad

    starts = jnp.arange(N_ROWS, dtype=jnp.int32) * ROW_DEV
    losses, grads = lax.map(one_block, starts)
    return losses.reshape(ROWS), grads.reshape(ROWS, STUDENT_BLOCKS * BLK)
```

```python
import functools

import jax
import jax.numpy as jnp
from jax import lax
from jax.experimental import pallas as pl
from jax.experimental.pallas import tpu as pltpu
from jax.sharding import PartitionSpec as P

CAP = 4
TEMP = 2.0
SHARE = 1.0 / 3.0
LANES = 128
MESH = pl.DeviceIdType.MESH


def iota(shape, dim):
    return lax.broadcasted_iota(jnp.int32, shape, dim)


def ones_where(mask):
    return jnp.where(mask, 1, 0)


def peer_of(me, k, n):
    out = 0
    bit = 1
    while bit < n:
        out = out + lax.rem(lax.div(me, bit) + (k // bit) % 2, 2) * bit
        bit *= 2
    return out


def pick_unroll(count):
    return max(u for u in range(1, 21) if count % u == 0)


def to_rows(columns, rows):
    lane = iota((rows, LANES), 1)
    grid = jnp.zeros((rows, LANES), jnp.float32)
    for k, column in enumerate(columns):
        grid = jnp.where(lane == k, column, grid)
    return grid.T[0:8]


def to_columns(row_block):
    return jnp.concatenate([row_block] * (LANES // 8), axis=0).T


def write_tables(n, span, block_counts, me, aligns, order_ref, meta_v, inv_v):
    width = n * span
    order_row = order_ref[...]
    hits = [a[:, 1:2] == order_row for a in aligns]
    present = sum(jnp.sum(ones_where(h), axis=0, keepdims=True) for h in hits)
    present = jnp.minimum(present, 1)
    down, across = iota((width, width), 0), iota((width, width), 1)
    present_col = jnp.sum(jnp.where(down == across, present, 0), axis=1, keepdims=True)
    owner_col = sum((ones_where(iota((width, 1), 0) >= o * span) for o in range(1, n)), jnp.zeros((width, 1), jnp.int32))
    owner_row = sum((ones_where(iota((1, width), 1) >= o * span) for o in range(1, n)), jnp.zeros((1, width), jnp.int32))
    earlier = (down < across) & (owner_col == owner_row)
    rank_row = jnp.sum(jnp.where(earlier, present_col, 0), axis=0, keepdims=True)
    slot_row = owner_row * CAP + rank_row
    inv_v[0] = jnp.zeros(inv_v.shape[1:], jnp.int32)
    meta_v[...] = jnp.zeros(meta_v.shape, jnp.int32)
    inv_v[0, 0:1, 0:width] = jnp.where(present > 0, jnp.minimum(rank_row, CAP), CAP)
    lanes = meta_v.shape[1]
    for t, (a, hit, blocks) in enumerate(zip(aligns, hits, block_counts)):
        count = a.shape[0]
        slot = jnp.sum(jnp.where(hit, slot_row, 0), axis=1, keepdims=True)
        down, across = iota((count, count), 0), iota((count, count), 1)
        slot_lane = jnp.sum(jnp.where(down == across, slot, 0), axis=0, keepdims=True)
        same_before = jnp.sum(
            ones_where((slot_lane == slot) & (across < down)), axis=1, keepdims=True
        )
        rank = same_before + jnp.sum(ones_where(slot_lane < slot), axis=1, keepdims=True)
        lane = iota((count, lanes), 1)
        place = rank == lane

        def by_rank(values):
            return jnp.sum(jnp.where(place, values, 0), axis=0, keepdims=True)

        meta_v[4 * t : 4 * t + 1, :] = by_rank(jnp.clip(a[:, 0:1] - me * blocks, 0, blocks - 1))
        meta_v[4 * t + 1 : 4 * t + 2, :] = by_rank(a[:, 2:3])
        meta_v[4 * t + 2 : 4 * t + 3, :] = by_rank(jnp.minimum(same_before, 1))
        upto = jnp.sum(ones_where(slot <= lane), axis=0, keepdims=True)
        here = jnp.sum(ones_where(slot == lane), axis=0, keepdims=True)
        meta_v[4 * t + 3 : 4 * t + 4, :] = jnp.where(here > 0, upto - 1, count)


def kernel(
    n, llama, qwen, gemma, student, al, aq, ag, tiles_hbm, order_ref,
    loss_ref, grad_ref,
    xl, xq, xg, xs, wl, wq, wg, pl_, pq, pg, tiles, meta_v, meta_s, inv_v, inv_s,
    stat, tot, crs, send, recv, in_sem, smem_sem, snd, rcv,
):
    me = lax.axis_index("vocab")
    rows = xs.shape[0]
    span = xs.shape[1] // LANES
    peers = [peer_of(me, k, n) for k in range(n)]
    order = [k for k in range(n - 1, 0, -1)]
    order.sort(key=lambda k: (k < n // 2, k))
    factor = n * span * LANES / TEMP

    raw = [xl, xq, xg]
    weights = [wl, wq, wg]
    prefix = [pl_, pq, pg]
    loads = [
        pltpu.make_async_copy(src, dst, in_sem.at[i])
        for i, (src, dst) in enumerate(
            [(llama, xl), (qwen, xq), (gemma, xg), (student, xs), (tiles_hbm, tiles)]
        )
    ]
    for load in loads:
        load.start()
    barrier = pltpu.get_barrier_semaphore()
    for k in range(1, n):
        pl.semaphore_signal(barrier, inc=1, device_id={"vocab": peers[k]}, device_id_type=MESH)

    aligns = [al[...], aq[...], ag[...]]
    block_counts = [x.shape[1] // LANES for x in raw]
    write_tables(n, span, block_counts, me, aligns, order_ref, meta_v, inv_v)
    meta_copy = pltpu.make_async_copy(meta_v, meta_s, smem_sem.at[0])
    meta_copy.start()
    for t in range(3):
        prefix[t][aligns[t].shape[0]] = jnp.zeros((rows, LANES), jnp.float32)
    for k in range(n):
        recv[k, CAP] = jnp.zeros((rows, LANES), jnp.bfloat16)

    def local_stats(x, w):
        blocks = x.shape[1] // LANES
        top = x[:, 0:LANES]
        for b in range(1, blocks):
            top = jnp.maximum(top, x[:, b * LANES : (b + 1) * LANES])
        top = jnp.max(top.astype(jnp.float32), axis=1, keepdims=True) / TEMP
        total = jnp.zeros((rows, LANES), jnp.float32)
        for b in range(blocks):
            e = jnp.exp(x[:, b * LANES : (b + 1) * LANES].astype(jnp.float32) / TEMP - top)
            total = total + e
            if w is not None:
                w[b] = e.astype(jnp.bfloat16)
        return top, jnp.sum(total, axis=1, keepdims=True)

    stats = []
    for t in range(3):
        loads[t].wait()
        stats.extend(local_stats(raw[t], weights[t]))
    loads[3].wait()
    stats.extend(local_stats(xs, None))
    stat[0] = to_rows(stats, rows)

    pl.semaphore_wait(barrier, n - 1)

    def remote(src, dst, kind, k):
        return pltpu.make_async_remote_copy(
            src_ref=src, dst_ref=dst, send_sem=snd.at[kind, k], recv_sem=rcv.at[kind, k],
            device_id={"vocab": peers[k]}, device_id_type=MESH,
        )

    stat_copies = [remote(stat.at[0], stat.at[k], 0, k) for k in order]
    inv_copies = [remote(inv_v.at[0], inv_v.at[k], 1, k) for k in order]
    for c in stat_copies + inv_copies:
        c.start()

    meta_copy.wait()
    loads[4].wait()
    for t in range(3):
        count = aligns[t].shape[0]
        unroll = pick_unroll(count)

        def step(i, acc, t=t, unroll=unroll):
            for u in range(unroll):
                p = i * unroll + u
                product = jnp.dot(
                    weights[t][meta_s[4 * t, p]],
                    tiles[meta_s[4 * t + 1, p]],
                    preferred_element_type=jnp.float32,
                )
                acc = jnp.where(meta_s[4 * t + 2, p] > 0, acc, 0.0) + product
                prefix[t][p] = acc
            return acc

        lax.fori_loop(0, count // unroll, step, jnp.zeros((rows, LANES), jnp.float32))

    for c in stat_copies:
        c.wait()
    mine = stat[0]
    scale_rows = []
    lse_row = None
    for t in range(4):
        peak = mine[2 * t : 2 * t + 1]
        for k in range(1, n):
            peak = jnp.maximum(peak, stat[k, 2 * t : 2 * t + 1])
        whole = jnp.zeros((1, rows), jnp.float32)
        for k in range(n):
            whole = whole + stat[k, 2 * t + 1 : 2 * t + 2] * jnp.exp(stat[k, 2 * t : 2 * t + 1] - peak)
        if t < 3:
            scale_rows.append(jnp.exp(mine[2 * t : 2 * t + 1] - peak) / whole * SHARE)
        else:
            lse_row = peak + jnp.log(whole)
    packed = to_columns(jnp.concatenate(scale_rows + [lse_row] + [jnp.zeros((4, rows), jnp.float32)], axis=0))
    scales = [packed[:, t : t + 1] for t in range(3)]
    lse = packed[:, 3:4]

    row_sum = jnp.zeros((rows, LANES), jnp.float32)
    data_copies = []
    for k in order + [0]:
        for j in range(CAP):
            s = peers[k] * CAP + j
            part = scales[0] * prefix[0][meta_s[3, s]]
            part = part + scales[1] * prefix[1][meta_s[7, s]]
            part = part + scales[2] * prefix[2][meta_s[11, s]]
            part = part.astype(jnp.bfloat16)
            row_sum = row_sum + part.astype(jnp.float32)
            if k == 0:
                recv[0, j] = part
            else:
                send[k, j] = part
        if k != 0:
            c = remote(send.at[k], recv.at[k, pl.ds(0, CAP)], 2, k)
            c.start()
            data_copies.append(c)
    tot[0] = to_rows([jnp.sum(row_sum, axis=1, keepdims=True)], rows)
    tot_copies = [remote(tot.at[0], tot.at[k], 3, k) for k in order]
    for c in tot_copies:
        c.start()
    for c in inv_copies:
        c.wait()
    inv_copy = pltpu.make_async_copy(inv_v, inv_s, smem_sem.at[1])
    inv_copy.start()
    inv_copy.wait()
    for c in tot_copies:
        c.wait()
    total_rows = sum(tot[k] for k in range(n))
    total = to_columns(total_rows)[:, 0:1]
    for c in data_copies:
        c.wait()

    cross = jnp.zeros((rows, LANES), jnp.float32)
    for b in range(span):
        target = jnp.zeros((rows, LANES), jnp.float32)
        for k in range(n):
            target = target + recv[k, inv_s[k, 0, me * span + b]].astype(jnp.float32)
        cols = slice(b * LANES, (b + 1) * LANES)
        scaled = xs[:, cols].astype(jnp.float32) / TEMP
        cross = cross + target * scaled
        grad_ref[:, cols] = (factor * (total * jnp.exp(scaled - lse) - target)).astype(jnp.bfloat16)
    crs[0] = to_rows([jnp.sum(cross, axis=1, keepdims=True)], rows)
    cross_copies = [remote(crs.at[0], crs.at[k], 4, k) for k in order]
    for c in cross_copies:
        c.start()
    for c in cross_copies:
        c.wait()
    cross_rows = sum(crs[k] for k in range(n))
    loss_ref[...] = total_rows[0:1] * lse_row - cross_rows[0:1]


def shards(llama, qwen, gemma, student, al, aq, ag, tiles, student_order):
    n = lax.axis_size("vocab")
    rows = student.shape[0]
    width = student_order.shape[0]
    aligns = (al, aq, ag)
    most = max([a.shape[0] for a in aligns] + [n * CAP])
    lanes = -(-most // LANES) * LANES
    inv_lanes = -(-width // LANES) * LANES
    logits = (llama, qwen, gemma, student)
    bf16, f32, i32 = jnp.bfloat16, jnp.float32, jnp.int32
    scratch = [pltpu.VMEM(x.shape, bf16) for x in logits]
    scratch += [pltpu.VMEM((x.shape[1] // LANES, rows, LANES), bf16) for x in logits[:3]]
    scratch += [pltpu.VMEM((a.shape[0] + 1, rows, LANES), f32) for a in aligns]
    scratch += [
        pltpu.VMEM(tiles.shape, bf16),
        pltpu.VMEM((16, lanes), i32),
        pltpu.SMEM((16, lanes), i32),
        pltpu.VMEM((n, 8, inv_lanes), i32),
        pltpu.SMEM((n, 8, inv_lanes), i32),
        pltpu.VMEM((n, 8, rows), f32),
        pltpu.VMEM((n, 8, rows), f32),
        pltpu.VMEM((n, 8, rows), f32),
        pltpu.VMEM((n, CAP, rows, LANES), bf16),
        pltpu.VMEM((n, CAP + 1, rows, LANES), bf16),
        pltpu.SemaphoreType.DMA((5,)),
        pltpu.SemaphoreType.DMA((2,)),
        pltpu.SemaphoreType.DMA((5, n)),
        pltpu.SemaphoreType.DMA((5, n)),
    ]
    hbm = pl.BlockSpec(memory_space=pl.ANY)
    vmem = pl.BlockSpec(memory_space=pltpu.VMEM)
    loss, grad = pl.pallas_call(
        functools.partial(kernel, n),
        out_shape=(
            jax.ShapeDtypeStruct((1, rows), f32),
            jax.ShapeDtypeStruct(student.shape, bf16),
        ),
        in_specs=[hbm] * 4 + [vmem] * 3 + [hbm, vmem],
        out_specs=(vmem, vmem),
        scratch_shapes=scratch,
        compiler_params=pltpu.CompilerParams(
            collective_id=0, has_side_effects=True, vmem_limit_bytes=52 * 2**20
        ),
    )(llama, qwen, gemma, student, al, aq, ag, tiles, student_order.reshape(1, width))
    return loss.reshape(rows), grad


def solution(mesh):
    wide = P(("groups", "rows"), "vocab")
    in_specs = (wide, wide, wide, wide, P("vocab", None), P("vocab", None), P("vocab", None), P(), P())
    out_specs = (P(("groups", "rows")), wide)
    return jax.shard_map(shards, mesh=mesh, in_specs=in_specs, out_specs=out_specs, check_vma=False)
```

```python
import functools

import jax
import jax.numpy as jnp
from jax import lax
from jax.experimental import pallas as pl
from jax.experimental.pallas import tpu as pltpu
from jax.sharding import PartitionSpec as P

CAP = 4
TEMP = 2.0
SHARE = 1.0 / 3.0
LANES = 128
MESH = pl.DeviceIdType.MESH


def iota(shape, dim):
    return lax.broadcasted_iota(jnp.int32, shape, dim)


def ones_where(mask):
    return jnp.where(mask, 1, 0)


def peer_of(me, k, n):
    out = 0
    bit = 1
    while bit < n:
        out = out + lax.rem(lax.div(me, bit) + (k // bit) % 2, 2) * bit
        bit *= 2
    return out


def pick_unroll(count):
    return max(u for u in range(1, 21) if count % u == 0)


def to_rows(columns, rows):
    lane = iota((rows, LANES), 1)
    grid = jnp.zeros((rows, LANES), jnp.float32)
    for k, column in enumerate(columns):
        grid = jnp.where(lane == k, column, grid)
    return grid.T[0:8]


def to_columns(row_block):
    return jnp.concatenate([row_block] * (LANES // 8), axis=0).T


def column_of(row):
    count = row.shape[1]
    square = (count, count)
    return jnp.sum(jnp.where(iota(square, 0) == iota(square, 1), row, 0), axis=1, keepdims=True)


def write_tables(n, span, block_counts, me, aligns, order_ref, meta_v, inv_v):
    width = n * span
    order_row = order_ref[...]
    entries = [[column_of(a[f : f + 1, :]) for f in range(3)] for a in aligns]
    hits = [e[1] == order_row for e in entries]
    present = sum(jnp.sum(ones_where(h), axis=0, keepdims=True) for h in hits)
    present = jnp.minimum(present, 1)
    down, across = iota((width, width), 0), iota((width, width), 1)
    present_col = jnp.sum(jnp.where(down == across, present, 0), axis=1, keepdims=True)
    owner_col = sum((ones_where(iota((width, 1), 0) >= o * span) for o in range(1, n)), jnp.zeros((width, 1), jnp.int32))
    owner_row = sum((ones_where(iota((1, width), 1) >= o * span) for o in range(1, n)), jnp.zeros((1, width), jnp.int32))
    earlier = (down < across) & (owner_col == owner_row)
    rank_row = jnp.sum(jnp.where(earlier, present_col, 0), axis=0, keepdims=True)
    slot_row = owner_row * CAP + rank_row
    inv_v[0] = jnp.zeros(inv_v.shape[1:], jnp.int32)
    meta_v[...] = jnp.zeros(meta_v.shape, jnp.int32)
    inv_v[0, 0:1, 0:width] = jnp.where(present > 0, jnp.minimum(rank_row, CAP), CAP)
    lanes = meta_v.shape[1]
    for t, (entry, hit, blocks) in enumerate(zip(entries, hits, block_counts)):
        count = hit.shape[0]
        slot = jnp.sum(jnp.where(hit, slot_row, 0), axis=1, keepdims=True)
        down, across = iota((count, count), 0), iota((count, count), 1)
        slot_lane = jnp.sum(jnp.where(down == across, slot, 0), axis=0, keepdims=True)
        same_before = jnp.sum(
            ones_where((slot_lane == slot) & (across < down)), axis=1, keepdims=True
        )
        rank = same_before + jnp.sum(ones_where(slot_lane < slot), axis=1, keepdims=True)
        lane = iota((count, lanes), 1)
        place = rank == lane

        def by_rank(values):
            return jnp.sum(jnp.where(place, values, 0), axis=0, keepdims=True)

        meta_v[4 * t : 4 * t + 1, :] = by_rank(jnp.clip(entry[0] - me * blocks, 0, blocks - 1))
        meta_v[4 * t + 1 : 4 * t + 2, :] = by_rank(entry[2])
        meta_v[4 * t + 2 : 4 * t + 3, :] = by_rank(jnp.minimum(same_before, 1))
        upto = jnp.sum(ones_where(slot <= lane), axis=0, keepdims=True)
        here = jnp.sum(ones_where(slot == lane), axis=0, keepdims=True)
        meta_v[4 * t + 3 : 4 * t + 4, :] = jnp.where(here > 0, upto - 1, count)


def kernel(
    n, llama, qwen, gemma, student, al_hbm, aq_hbm, ag_hbm, tiles_hbm, order_hbm,
    loss_ref, grad_ref,
    al, aq, ag, order_ref, xl, xq, xg, xs, wl, wq, wg, pl_, pq, pg, tiles, meta_v, meta_s, inv_v, inv_s,
    stat, tot, crs, target, soft, send, *more,
):
    recv = more[:n]
    in_sem, smem_sem, snd, rcv = more[n:]
    me = lax.axis_index("vocab")
    rows = xs.shape[0]
    span = xs.shape[1] // LANES
    peers = [peer_of(me, k, n) for k in range(n)]
    order = [k for k in range(n - 1, 0, -1)]
    order.sort(key=lambda k: (k < n // 2, k))
    factor = n * span * LANES / TEMP

    raw = [xl, xq, xg]
    weights = [wl, wq, wg]
    prefix = [pl_, pq, pg]
    loads = [
        pltpu.make_async_copy(src, dst, in_sem.at[i])
        for i, (src, dst) in enumerate(
            [
                (al_hbm, al), (aq_hbm, aq), (ag_hbm, ag), (order_hbm, order_ref),
                (llama, xl), (qwen, xq), (gemma, xg), (student, xs), (tiles_hbm, tiles),
            ]
        )
    ]
    barrier = pltpu.get_barrier_semaphore()
    for k in range(1, n):
        pl.semaphore_signal(barrier, inc=1, device_id={"vocab": peers[k]}, device_id_type=MESH)
    for load in loads:
        load.start()
    for load in loads[:4]:
        load.wait()
    loads = loads[4:]

    aligns = [al[...], aq[...], ag[...]]
    block_counts = [x.shape[1] // LANES for x in raw]
    write_tables(n, span, block_counts, me, aligns, order_ref, meta_v, inv_v)
    meta_copy = pltpu.make_async_copy(meta_v, meta_s, smem_sem.at[0])
    meta_copy.start()
    for t in range(3):
        prefix[t][aligns[t].shape[1]] = jnp.zeros((rows, LANES), jnp.float32)
    for k in range(n):
        recv[k][CAP] = jnp.zeros((rows, LANES), jnp.bfloat16)

    def local_stats(x, w):
        blocks = x.shape[1] // LANES
        top = x[:, 0:LANES]
        for b in range(1, blocks):
            top = jnp.maximum(top, x[:, b * LANES : (b + 1) * LANES])
        top = jnp.max(top.astype(jnp.float32), axis=1, keepdims=True) / TEMP
        total = jnp.zeros((rows, LANES), jnp.float32)
        for b in range(blocks):
            e = jnp.exp(x[:, b * LANES : (b + 1) * LANES].astype(jnp.float32) / TEMP - top)
            total = total + e
            if w is not None:
                w[b] = e.astype(jnp.bfloat16)
        return top, jnp.sum(total, axis=1, keepdims=True)

    stats = []
    for t in range(3):
        loads[t].wait()
        stats.extend(local_stats(raw[t], weights[t]))
    stat[0] = to_rows(stats, rows)

    pl.semaphore_wait(barrier, n - 1)

    def remote(src, dst, kind, k):
        return pltpu.make_async_remote_copy(
            src_ref=src, dst_ref=dst, send_sem=snd.at[kind, k], recv_sem=rcv.at[kind, k],
            device_id={"vocab": peers[k]}, device_id_type=MESH,
        )

    stat_copies = [remote(stat.at[0], stat.at[k], 0, k) for k in order]
    inv_copies = [remote(inv_v.at[0], inv_v.at[k], 1, k) for k in order]
    for c in stat_copies + inv_copies:
        c.start()

    loads[3].wait()
    student_stats = local_stats(xs, None)
    meta_copy.wait()
    loads[4].wait()
    for t in range(3):
        count = aligns[t].shape[1]
        unroll = pick_unroll(count)

        def step(i, acc, t=t, unroll=unroll):
            for u in range(unroll):
                p = i * unroll + u
                product = jnp.dot(
                    weights[t][meta_s[4 * t, p]],
                    tiles[meta_s[4 * t + 1, p]],
                    preferred_element_type=jnp.float32,
                )
                acc = jnp.where(meta_s[4 * t + 2, p] > 0, acc, 0.0) + product
                prefix[t][p] = acc
            return acc

        lax.fori_loop(0, count // unroll, step, jnp.zeros((rows, LANES), jnp.float32))

    for c in stat_copies:
        c.wait()

    def combine(ref, at):
        peak = ref[0, at : at + 1]
        for k in range(1, n):
            peak = jnp.maximum(peak, ref[k, at : at + 1])
        whole = jnp.zeros((1, rows), jnp.float32)
        for k in range(n):
            whole = whole + ref[k, at + 1 : at + 2] * jnp.exp(ref[k, at : at + 1] - peak)
        return peak, whole

    scale_rows = []
    for t in range(3):
        peak, whole = combine(stat, 2 * t)
        scale_rows.append(jnp.exp(stat[0, 2 * t : 2 * t + 1] - peak) / whole * SHARE)
    packed = to_columns(jnp.concatenate(scale_rows + [jnp.zeros((5, rows), jnp.float32)], axis=0))
    scales = [packed[:, t : t + 1] for t in range(3)]

    row_sum = jnp.zeros((rows, LANES), jnp.float32)
    data_copies = []
    for k in order + [0]:
        for j in range(CAP):
            s = peers[k] * CAP + j
            part = scales[0] * prefix[0][meta_s[3, s]]
            part = part + scales[1] * prefix[1][meta_s[7, s]]
            part = part + scales[2] * prefix[2][meta_s[11, s]]
            part = part.astype(jnp.bfloat16)
            row_sum = row_sum + part.astype(jnp.float32)
            if k == 0:
                recv[0][j] = part
            else:
                send[k, j] = part
        if k != 0:
            c = remote(send.at[k], recv[k].at[pl.ds(0, CAP)], 2, k)
            c.start()
            data_copies.append(c)
    tot[0] = to_rows([*student_stats, jnp.sum(row_sum, axis=1, keepdims=True)], rows)
    tot_copies = [remote(tot.at[0], tot.at[k], 3, k) for k in order]
    for c in tot_copies:
        c.start()
    for c in inv_copies:
        c.wait()
    inv_copy = pltpu.make_async_copy(inv_v, inv_s, smem_sem.at[1])
    inv_copy.start()
    inv_copy.wait()

    def columns(b):
        return slice(b * LANES, (b + 1) * LANES)

    def land(k, cross):
        for b in range(span):
            block = recv[k][inv_s[k, 0, me * span + b]].astype(jnp.float32)
            cross = cross + block * (xs[:, columns(b)].astype(jnp.float32) / TEMP)
            target[b] = block if k == 0 else target[b] + block
        return cross

    cross = land(0, jnp.zeros((rows, LANES), jnp.float32))
    for c in tot_copies:
        c.wait()
    student_peak, student_total = combine(tot, 0)
    lse_row = student_peak + jnp.log(student_total)
    total_row = sum(tot[k, 2:3] for k in range(n))
    packed = to_columns(jnp.concatenate([lse_row, total_row, jnp.zeros((6, rows), jnp.float32)], axis=0))
    lse, total = packed[:, 0:1], packed[:, 1:2]
    for b in range(span):
        soft[b] = total * jnp.exp(xs[:, columns(b)].astype(jnp.float32) / TEMP - lse)
    for k, c in zip(order, data_copies):
        c.wait()
        cross = land(k, cross)
    crs[0] = to_rows([jnp.sum(cross, axis=1, keepdims=True)], rows)
    cross_copies = [remote(crs.at[0], crs.at[k], 4, k) for k in order]
    for c in cross_copies:
        c.start()
    for b in range(span):
        grad_ref[:, columns(b)] = (factor * (soft[b] - target[b])).astype(jnp.bfloat16)
    for c in cross_copies:
        c.wait()
    loss_ref[...] = total_row * lse_row - sum(crs[k, 0:1] for k in range(n))


def shards(llama, qwen, gemma, student, al, aq, ag, tiles, student_order):
    n = lax.axis_size("vocab")
    rows = student.shape[0]
    width = student_order.shape[0]
    aligns = (al, aq, ag)
    most = max([a.shape[0] for a in aligns] + [n * CAP])
    lanes = -(-most // LANES) * LANES
    inv_lanes = -(-width // LANES) * LANES
    logits = (llama, qwen, gemma, student)
    bf16, f32, i32 = jnp.bfloat16, jnp.float32, jnp.int32
    scratch = [pltpu.VMEM(a.shape[::-1], i32) for a in aligns] + [pltpu.VMEM((1, width), i32)]
    scratch += [pltpu.VMEM(x.shape, bf16) for x in logits]
    scratch += [pltpu.VMEM((x.shape[1] // LANES, rows, LANES), bf16) for x in logits[:3]]
    scratch += [pltpu.VMEM((a.shape[0] + 1, rows, LANES), f32) for a in aligns]
    scratch += [
        pltpu.VMEM(tiles.shape, bf16),
        pltpu.VMEM((16, lanes), i32),
        pltpu.SMEM((16, lanes), i32),
        pltpu.VMEM((n, 8, inv_lanes), i32),
        pltpu.SMEM((n, 8, inv_lanes), i32),
        pltpu.VMEM((n, 8, rows), f32),
        pltpu.VMEM((n, 8, rows), f32),
        pltpu.VMEM((n, 8, rows), f32),
        pltpu.VMEM((student.shape[1] // LANES, rows, LANES), f32),
        pltpu.VMEM((student.shape[1] // LANES, rows, LANES), f32),
        pltpu.VMEM((n, CAP, rows, LANES), bf16),
    ]
    scratch += [pltpu.VMEM((CAP + 1, rows, LANES), bf16) for _ in range(n)]
    scratch += [
        pltpu.SemaphoreType.DMA((9,)),
        pltpu.SemaphoreType.DMA((2,)),
        pltpu.SemaphoreType.DMA((5, n)),
        pltpu.SemaphoreType.DMA((5, n)),
    ]
    hbm = pl.BlockSpec(memory_space=pltpu.HBM)
    vmem = pl.BlockSpec(memory_space=pltpu.VMEM)
    loss, grad = pl.pallas_call(
        functools.partial(kernel, n),
        out_shape=(
            jax.ShapeDtypeStruct((1, rows), f32),
            jax.ShapeDtypeStruct(student.shape, bf16),
        ),
        in_specs=[hbm] * 9,
        out_specs=(vmem, vmem),
        scratch_shapes=scratch,
        compiler_params=pltpu.CompilerParams(
            collective_id=0, has_side_effects=True, vmem_limit_bytes=60 * 2**20
        ),
    )(llama, qwen, gemma, student, al.T, aq.T, ag.T, tiles, student_order.reshape(1, width))
    return loss.reshape(rows), grad


def solution(mesh):
    wide = P(("groups", "rows"), "vocab")
    in_specs = (wide, wide, wide, wide, P("vocab", None), P("vocab", None), P("vocab", None), P(), P())
    out_specs = (P(("groups", "rows")), wide)
    return jax.shard_map(shards, mesh=mesh, in_specs=in_specs, out_specs=out_specs, check_vma=False)
```

```python
import functools

import jax
import jax.numpy as jnp
from jax import lax
from jax.experimental import pallas as pl
from jax.experimental.pallas import tpu as pltpu
from jax.sharding import PartitionSpec as P

CAP = 4
TEMP = 2.0
SHARE = 1.0 / 3.0
LANES = 128
MESH = pl.DeviceIdType.MESH


def iota(shape, dim):
    return lax.broadcasted_iota(jnp.int32, shape, dim)


def ones_where(mask):
    return jnp.where(mask, 1, 0)


def peer_of(me, k, n):
    out = 0
    bit = 1
    while bit < n:
        out = out + lax.rem(lax.div(me, bit) + (k // bit) % 2, 2) * bit
        bit *= 2
    return out


def pick_unroll(count):
    return max(u for u in range(1, 21) if count % u == 0)


def to_rows(columns, rows):
    lane = iota((rows, LANES), 1)
    grid = jnp.zeros((rows, LANES), jnp.float32)
    for k, column in enumerate(columns):
        grid = jnp.where(lane == k, column, grid)
    return grid.T[0:8]


def to_columns(row_block):
    return jnp.concatenate([row_block] * (LANES // 8), axis=0).T


def column_of(row):
    count = row.shape[1]
    square = (count, count)
    return jnp.sum(jnp.where(iota(square, 0) == iota(square, 1), row, 0), axis=1, keepdims=True)


def write_tables(n, span, block_counts, me, aligns, order_ref, meta_v, inv_v):
    width = n * span
    order_row = order_ref[...]
    entries = [[column_of(a[f : f + 1, :]) for f in range(3)] for a in aligns]
    hits = [e[1] == order_row for e in entries]
    present = sum(jnp.sum(ones_where(h), axis=0, keepdims=True) for h in hits)
    present = jnp.minimum(present, 1)
    down, across = iota((width, width), 0), iota((width, width), 1)
    present_col = jnp.sum(jnp.where(down == across, present, 0), axis=1, keepdims=True)
    owner_col = sum((ones_where(iota((width, 1), 0) >= o * span) for o in range(1, n)), jnp.zeros((width, 1), jnp.int32))
    owner_row = sum((ones_where(iota((1, width), 1) >= o * span) for o in range(1, n)), jnp.zeros((1, width), jnp.int32))
    earlier = (down < across) & (owner_col == owner_row)
    rank_row = jnp.sum(jnp.where(earlier, present_col, 0), axis=0, keepdims=True)
    slot_row = owner_row * CAP + rank_row
    inv_v[0] = jnp.zeros(inv_v.shape[1:], jnp.int32)
    meta_v[...] = jnp.zeros(meta_v.shape, jnp.int32)
    inv_v[0, 0:1, 0:width] = jnp.where(present > 0, jnp.minimum(rank_row, CAP), CAP)
    lanes = meta_v.shape[1]
    for t, (entry, hit, blocks) in enumerate(zip(entries, hits, block_counts)):
        count = hit.shape[0]
        slot = jnp.sum(jnp.where(hit, slot_row, 0), axis=1, keepdims=True)
        down, across = iota((count, count), 0), iota((count, count), 1)
        slot_lane = jnp.sum(jnp.where(down == across, slot, 0), axis=0, keepdims=True)
        same_before = jnp.sum(
            ones_where((slot_lane == slot) & (across < down)), axis=1, keepdims=True
        )
        rank = same_before + jnp.sum(ones_where(slot_lane < slot), axis=1, keepdims=True)
        lane = iota((count, lanes), 1)
        place = rank == lane

        def by_rank(values):
            return jnp.sum(jnp.where(place, values, 0), axis=0, keepdims=True)

        meta_v[4 * t : 4 * t + 1, :] = by_rank(jnp.clip(entry[0] - me * blocks, 0, blocks - 1))
        meta_v[4 * t + 1 : 4 * t + 2, :] = by_rank(entry[2])
        meta_v[4 * t + 2 : 4 * t + 3, :] = by_rank(jnp.minimum(same_before, 1))
        upto = jnp.sum(ones_where(slot <= lane), axis=0, keepdims=True)
        here = jnp.sum(ones_where(slot == lane), axis=0, keepdims=True)
        meta_v[4 * t + 3 : 4 * t + 4, :] = jnp.where(here > 0, upto - 1, count)


def kernel(
    n, llama, qwen, gemma, student, al_hbm, aq_hbm, ag_hbm, tiles_hbm, order_hbm,
    loss_ref, grad_ref,
    al, aq, ag, order_ref, xl, xq, xg, xs, wl, wq, wg, pl_, pq, pg, tiles, meta_v, meta_s, inv_v, inv_s,
    stat, tot, crs, target, soft, send, *more,
):
    recv = more[:n]
    in_sem, smem_sem, snd, rcv = more[n:]
    me = lax.axis_index("vocab")
    rows = xs.shape[0]
    span = xs.shape[1] // LANES
    peers = [peer_of(me, k, n) for k in range(n)]
    order = [k for k in range(n - 1, 0, -1)]
    order.sort(key=lambda k: (k < n // 2, k))
    factor = n * span * LANES / TEMP

    raw = [xl, xq, xg]
    weights = [wl, wq, wg]
    prefix = [pl_, pq, pg]
    loads = [
        pltpu.make_async_copy(src, dst, in_sem.at[i])
        for i, (src, dst) in enumerate(
            [
                (al_hbm, al), (aq_hbm, aq), (ag_hbm, ag), (order_hbm, order_ref),
                (llama, xl), (qwen, xq), (gemma, xg), (student, xs), (tiles_hbm, tiles),
            ]
        )
    ]
    barrier = pltpu.get_barrier_semaphore()
    for k in range(1, n):
        pl.semaphore_signal(barrier, inc=1, device_id={"vocab": peers[k]}, device_id_type=MESH)
    for load in loads:
        load.start()
    for load in loads[:4]:
        load.wait()
    loads = loads[4:]

    aligns = [al[...], aq[...], ag[...]]
    block_counts = [x.shape[1] // LANES for x in raw]
    write_tables(n, span, block_counts, me, aligns, order_ref, meta_v, inv_v)
    meta_copy = pltpu.make_async_copy(meta_v, meta_s, smem_sem.at[0])
    meta_copy.start()
    for t in range(3):
        prefix[t][aligns[t].shape[1]] = jnp.zeros((rows, LANES), jnp.float32)
    for k in range(n):
        recv[k][CAP] = jnp.zeros((rows, LANES), jnp.bfloat16)

    def local_stats(x, w):
        blocks = x.shape[1] // LANES
        top = x[:, 0:LANES]
        for b in range(1, blocks):
            top = jnp.maximum(top, x[:, b * LANES : (b + 1) * LANES])
        top = jnp.max(top.astype(jnp.float32), axis=1, keepdims=True) / TEMP
        total = jnp.zeros((rows, LANES), jnp.float32)
        for b in range(blocks):
            e = jnp.exp(x[:, b * LANES : (b + 1) * LANES].astype(jnp.float32) / TEMP - top)
            total = total + e
            if w is not None:
                w[b] = e.astype(jnp.bfloat16)
        return top, jnp.sum(total, axis=1, keepdims=True)

    stats = []
    for t in range(3):
        loads[t].wait()
        stats.extend(local_stats(raw[t], weights[t]))
    stat[0] = to_rows(stats, rows)

    pl.semaphore_wait(barrier, n - 1)

    def remote(src, dst, kind, k):
        return pltpu.make_async_remote_copy(
            src_ref=src, dst_ref=dst, send_sem=snd.at[kind, k], recv_sem=rcv.at[kind, k],
            device_id={"vocab": peers[k]}, device_id_type=MESH,
        )

    stat_copies = [remote(stat.at[0], stat.at[k], 0, k) for k in order]
    inv_copies = [remote(inv_v.at[0], inv_v.at[k], 1, k) for k in order]
    for c in stat_copies + inv_copies:
        c.start()

    loads[3].wait()
    student_stats = local_stats(xs, None)
    meta_copy.wait()
    loads[4].wait()
    for t in range(3):
        count = aligns[t].shape[1]
        unroll = pick_unroll(count)

        def step(i, acc, t=t, unroll=unroll):
            for u in range(unroll):
                p = i * unroll + u
                product = jnp.dot(
                    weights[t][meta_s[4 * t, p]],
                    tiles[meta_s[4 * t + 1, p]],
                    preferred_element_type=jnp.float32,
                )
                acc = jnp.where(meta_s[4 * t + 2, p] > 0, acc, 0.0) + product
                prefix[t][p] = acc
            return acc

        lax.fori_loop(0, count // unroll, step, jnp.zeros((rows, LANES), jnp.float32))

    for c in stat_copies:
        c.wait()

    def combine(ref, at):
        peak = ref[0, at : at + 1]
        for k in range(1, n):
            peak = jnp.maximum(peak, ref[k, at : at + 1])
        whole = jnp.zeros((1, rows), jnp.float32)
        for k in range(n):
            whole = whole + ref[k, at + 1 : at + 2] * jnp.exp(ref[k, at : at + 1] - peak)
        return peak, whole

    scale_rows = []
    for t in range(3):
        peak, whole = combine(stat, 2 * t)
        scale_rows.append(jnp.exp(stat[0, 2 * t : 2 * t + 1] - peak) / whole * SHARE)
    packed = to_columns(jnp.concatenate(scale_rows + [jnp.zeros((5, rows), jnp.float32)], axis=0))
    scales = [packed[:, t : t + 1] for t in range(3)]

    row_sum = jnp.zeros((rows, LANES), jnp.float32)
    data_copies = []
    for k in order + [0]:
        for j in range(CAP):
            s = peers[k] * CAP + j
            part = scales[0] * prefix[0][meta_s[3, s]]
            part = part + scales[1] * prefix[1][meta_s[7, s]]
            part = part + scales[2] * prefix[2][meta_s[11, s]]
            part = part.astype(jnp.bfloat16)
            row_sum = row_sum + part.astype(jnp.float32)
            if k == 0:
                recv[0][j] = part
            else:
                send[k, j] = part
        if k != 0:
            c = remote(send.at[k], recv[k].at[pl.ds(0, CAP)], 2, k)
            c.start()
            data_copies.append(c)
    tot[0] = to_rows([*student_stats, jnp.sum(row_sum, axis=1, keepdims=True)], rows)
    tot_copies = [remote(tot.at[0], tot.at[k], 3, k) for k in order]
    for c in tot_copies:
        c.start()
    for c in inv_copies:
        c.wait()
    inv_copy = pltpu.make_async_copy(inv_v, inv_s, smem_sem.at[1])
    inv_copy.start()
    inv_copy.wait()

    def columns(b):
        return slice(b * LANES, (b + 1) * LANES)

    def land(k, cross):
        for b in range(span):
            block = recv[k][inv_s[k, 0, me * span + b]].astype(jnp.float32)
            cross = cross + block * (xs[:, columns(b)].astype(jnp.float32) / TEMP)
            target[b] = block if k == 0 else target[b] + block
        return cross

    cross = land(0, jnp.zeros((rows, LANES), jnp.float32))
    for c in tot_copies:
        c.wait()
    student_peak, student_total = combine(tot, 0)
    lse_row = student_peak + jnp.log(student_total)
    total_row = sum(tot[k, 2:3] for k in range(n))
    packed = to_columns(jnp.concatenate([lse_row, total_row, jnp.zeros((6, rows), jnp.float32)], axis=0))
    lse, total = packed[:, 0:1], packed[:, 1:2]
    for b in range(span):
        soft[b] = total * jnp.exp(xs[:, columns(b)].astype(jnp.float32) / TEMP - lse)
    for k, c in zip(order, data_copies):
        c.wait()
        cross = land(k, cross)
    crs[0] = to_rows([jnp.sum(cross, axis=1, keepdims=True)], rows)
    cross_copies = [remote(crs.at[0], crs.at[k], 4, k) for k in order]
    for c in cross_copies:
        c.start()
    for b in range(span):
        grad_ref[:, columns(b)] = (factor * (soft[b] - target[b])).astype(jnp.bfloat16)
    for c in cross_copies:
        c.wait()
    loss_ref[...] = total_row * lse_row - sum(crs[k, 0:1] for k in range(n))


def shards(llama, qwen, gemma, student, al, aq, ag, tiles, student_order):
    n = lax.axis_size("vocab")
    rows = student.shape[0]
    width = student_order.shape[0]
    aligns = (al, aq, ag)
    most = max([a.shape[0] for a in aligns] + [n * CAP])
    lanes = -(-most // LANES) * LANES
    inv_lanes = -(-width // LANES) * LANES
    logits = (llama, qwen, gemma, student)
    bf16, f32, i32 = jnp.bfloat16, jnp.float32, jnp.int32
    scratch = [pltpu.VMEM(a.shape[::-1], i32) for a in aligns] + [pltpu.VMEM((1, width), i32)]
    scratch += [pltpu.VMEM(x.shape, bf16) for x in logits]
    scratch += [pltpu.VMEM((x.shape[1] // LANES, rows, LANES), bf16) for x in logits[:3]]
    scratch += [pltpu.VMEM((a.shape[0] + 1, rows, LANES), f32) for a in aligns]
    scratch += [
        pltpu.VMEM(tiles.shape, bf16),
        pltpu.VMEM((16, lanes), i32),
        pltpu.SMEM((16, lanes), i32),
        pltpu.VMEM((n, 8, inv_lanes), i32),
        pltpu.SMEM((n, 8, inv_lanes), i32),
        pltpu.VMEM((n, 8, rows), f32),
        pltpu.VMEM((n, 8, rows), f32),
        pltpu.VMEM((n, 8, rows), f32),
        pltpu.VMEM((student.shape[1] // LANES, rows, LANES), f32),
        pltpu.VMEM((student.shape[1] // LANES, rows, LANES), f32),
        pltpu.VMEM((n, CAP, rows, LANES), bf16),
    ]
    scratch += [pltpu.VMEM((CAP + 1, rows, LANES), bf16) for _ in range(n)]
    scratch += [
        pltpu.SemaphoreType.DMA((9,)),
        pltpu.SemaphoreType.DMA((2,)),
        pltpu.SemaphoreType.DMA((5, n)),
        pltpu.SemaphoreType.DMA((5, n)),
    ]
    hbm = pl.BlockSpec(memory_space=pltpu.HBM)
    vmem = pl.BlockSpec(memory_space=pltpu.VMEM)
    loss, grad = pl.pallas_call(
        functools.partial(kernel, n),
        out_shape=(
            pltpu.VMEM((1, rows), f32),
            pltpu.VMEM(student.shape, bf16),
        ),
        in_specs=[hbm] * 9,
        out_specs=(vmem, vmem),
        scratch_shapes=scratch,
        compiler_params=pltpu.CompilerParams(
            collective_id=0, has_side_effects=True, vmem_limit_bytes=60 * 2**20
        ),
    )(llama, qwen, gemma, student, al.T, aq.T, ag.T, tiles, student_order.reshape(1, width))
    return loss.reshape(rows), grad


def solution(mesh):
    wide = P(("groups", "rows"), "vocab")
    in_specs = (wide, wide, wide, wide, P("vocab", None), P("vocab", None), P("vocab", None), P(), P())
    out_specs = (P(("groups", "rows")), wide)
    return jax.shard_map(shards, mesh=mesh, in_specs=in_specs, out_specs=out_specs, check_vma=False)
```
